256 devices in a mesh: col: 64 (over y, z, x_lo), row: 4 (over x_hi, core).
Axes of the slice: x: 4 (x_hi: 2, x_lo: 2; x = x_hi * 2 + x_lo), y: 4, z: 8, core: 2. Of those that a mesh axis runs over, the one named last changes fastest.
Arguments:
- matrix: float32 [2048, 32768], P('row', 'col'), may hold values from -0.6 to 0.6
- lower_inverses: float32 [2, 512, 512], replicated, as said below
- upper_inverses: float32 [2, 512, 512], replicated, as said below
- pivots: int32 [2, 512], replicated, may hold values from 0 to 2047, as said below
Outputs:
- factored: float32 [2048, 32768], P('row', 'col')
The draws below stay inside these ranges and needn't reach their ends.
Inputs may be any that keep to these rules, and one draw needn't show every extreme that they name: `pivots`: in panel p, entry j is either p * 512 + j (no exchange) or a row at or beyond (p + 1) * 512; the entries of one panel that differ from p * 512 + j are distinct. `lower_inverses`: each matrix is unit lower triangular. `upper_inverses`: each matrix is upper triangular.
All inputs are finite; a program needn't handle non-finite values.
Results may differ from the reference program's by a relative error of at most 0.00011.
Values sent between devices are 32-bit elements; how exact they have to be, the bound alone decides.
A program may use at most 64 MiB of HBM per device.

```python
import jax
import jax.numpy as jnp
from jax import lax

PW = 512
PANELS = 2
N = 32768
M = 2048


def draw_lower_inverses(key, part):
    entries = jax.random.normal(key, (PANELS, PW, PW), jnp.float32)
    rows_idx = jnp.arange(PW)[:, None]
    cols_idx = jnp.arange(PW)[None, :]
    strict = (rows_idx > cols_idx).astype(jnp.float32)
    ident = (rows_idx == cols_idx).astype(jnp.float32)
    return entries * strict[None] * (0.5 / PW ** 0.5) + ident[None]


def draw_upper_inverses(key, part):
    entries = jax.random.normal(jax.random.fold_in(key, 5), (PANELS, PW, PW), jnp.float32)
    diagonal = jax.random.uniform(jax.random.fold_in(key, 6), (PANELS, PW), jnp.float32, 0.6, 1.4)
    rows_idx = jnp.arange(PW)[:, None]
    cols_idx = jnp.arange(PW)[None, :]
    strict = (rows_idx < cols_idx).astype(jnp.float32)
    ident = (rows_idx == cols_idx).astype(jnp.float32)
    return entries * strict[None] * (0.5 / PW ** 0.5) + ident[None] * diagonal[:, :, None]


def draw_pivots(key, part):
    positions = jnp.arange(PW, dtype=jnp.int32)
    result_rows = []
    for panel_step in range(PANELS):
        offset = panel_step * PW
        if panel_step == 0:
            chosen = jax.random.permutation(jax.random.fold_in(key, 11), M - PW - 1)[:PW].astype(jnp.int32) + PW
        else:
            chosen = jax.random.permutation(jax.random.fold_in(key, 11 + panel_step), M - offset - PW)[:PW].astype(jnp.int32) + offset + PW
        fixed_rows = jax.random.randint(jax.random.fold_in(key, 31 + panel_step), (PW,), 0, 8) == 0
        if panel_step == 0:
            fixed_rows = fixed_rows.at[0].set(True)
        chosen = jnp.where(fixed_rows, offset + positions, chosen)
        if panel_step == 0:
            chosen = chosen.at[PW - 1].set(M - 1)
        result_rows.append(chosen)
    return jnp.stack(result_rows).astype(jnp.int32)


def shard_levels(key, shape, pieces, least, largest):
    def one(axis_at, shards_of):
        heights = jax.random.uniform(jax.random.fold_in(jax.random.fold_in(key, 6), axis_at), (shards_of,), jnp.float32, least / len(pieces), largest / len(pieces))
        return jnp.repeat(jnp.exp(heights), shape[axis_at] // shards_of).reshape((-1,) + (1,) * (len(shape) - axis_at - 1))

    gain = one(*pieces[0])
    for cut in pieces[1:]:
        gain = gain * one(*cut)
    return gain


def normal_values(stream_key, dims, deviation, bound, shards=(), kind=jnp.bfloat16):
    gain = shard_levels(stream_key, dims, shards, -0.22, 0.18) if shards else 1.0
    result = jax.random.normal(stream_key, dims, jnp.float32) * deviation * gain
    return jnp.minimum(jnp.maximum(result, -bound), bound).astype(kind)


def setup_inputs(seed: int = 0) -> dict:
    splits = jax.random.split(jax.random.key(seed), 5)
    return {
        "matrix": normal_values(splits[0], (M, N), 0.1, 0.6, ((0, 4), (1, 64)), jnp.float32),
        "lower_inverses": draw_lower_inverses(jax.random.fold_in(splits[4], 71), 0),
        "upper_inverses": draw_upper_inverses(jax.random.fold_in(splits[4], 71), 0),
        "pivots": draw_pivots(jax.random.fold_in(splits[4], 71), 0),
    }


def reference(matrix, lower_inverses, upper_inverses, pivots):
    current = matrix
    all_rows = jnp.arange(M, dtype=jnp.int32)
    all_cols = jnp.arange(N, dtype=jnp.int32)
    for panel_step in range(PANELS):
        offset = panel_step * PW
        pivot_rows = pivots[panel_step].astype(jnp.int32)
        block_rows = offset + jnp.arange(PW, dtype=jnp.int32)
        fixed_rows = pivot_rows == block_rows
        sources = jnp.concatenate([pivot_rows, block_rows])
        targets = jnp.concatenate([block_rows, jnp.where(fixed_rows, M, pivot_rows)])
        moved_rows = current[sources]
        top_rows = moved_rows[:PW]
        column_mask = all_cols >= offset + PW
        upper_rows = jnp.dot(lower_inverses[panel_step], top_rows, precision=lax.Precision.HIGHEST)
        upper_used = jnp.where(column_mask[None, :], upper_rows, 0.0)
        new_rows = jnp.concatenate([jnp.where(column_mask[None, :], upper_rows, top_rows), moved_rows[PW:]])
        current = current.at[targets].set(new_rows, mode="drop")
        panel_cols = current[:, offset:offset + PW]
        lower_cols = jnp.dot(panel_cols, upper_inverses[panel_step], precision=lax.Precision.HIGHEST)
        lower_mask = all_rows >= offset + PW
        lower_used = jnp.where(lower_mask[:, None], lower_cols, 0.0)
        current = current - jnp.dot(lower_used, upper_used, precision=lax.Precision.HIGHEST)
        current = current.at[:, offset:offset + PW].set(jnp.where(lower_mask[:, None], lower_cols, panel_cols))
    return current
```

```python
import functools

import jax
import jax.numpy as jnp
from jax import lax
from jax.experimental import pallas as pl
from jax.experimental.pallas import tpu as pltpu
from jax.sharding import PartitionSpec as P

MESH = pl.DeviceIdType.MESH
PW = 512
NX, NY, NZ = 4, 4, 8
PIECE = 16
CHUNKS = 4
F32 = jnp.float32
BF16 = jnp.bfloat16


def split(value):
    high = value.astype(BF16)
    return high, (value - high.astype(F32)).astype(BF16)


def dot(a, b):
    return jnp.dot(a, b, preferred_element_type=F32)


def dot3(a, b):
    ah, al = split(a)
    bh, bl = split(b)
    return dot(ah, bh) + (dot(ah, bl) + dot(al, bh))


def device(x, y, z, core):
    return ((y * NZ + z) * 2 + lax.rem(x, 2), (x // 2) * 2 + core)


def wrap(value, size):
    return lax.rem(value + size, size)


def remote(src, dst, send, recv, target):
    return pltpu.make_async_remote_copy(
        src_ref=src, dst_ref=dst, send_sem=send, recv_sem=recv, device_id=target, device_id_type=MESH
    )


def column(row):
    shape = (PW, PW)
    eye = lax.broadcasted_iota(jnp.int32, shape, 0) == lax.broadcasted_iota(jnp.int32, shape, 1)
    return jnp.sum(jnp.where(eye, row, 0.0), axis=1, keepdims=True)


def swapped(rows, pivot_row, offset):
    lane = lax.broadcasted_iota(jnp.int32, (PW, PW), 1).astype(F32) + offset
    return rows + jnp.sum(jnp.where(pivot_row == rows, lane - rows, 0.0), axis=1, keepdims=True)


def kernel(
    a_ref, lower_ref, upper_ref, pivots_ref, o_ref,
    pan, own, acc_a, acc_b, acc_c, acc_d,
    s1_send, s1_recv, sx_send, sx_recv, sz_send, sy_send, unit_recv, swap_send, swap_recv,
    e1_send, e1_recv, e2_send, e2_recv, e3_send, e3_recv, local_sem,
):
    col = lax.axis_index("col")
    row = lax.axis_index("row")
    core = lax.rem(row, 2)
    xh = row // 2
    x = xh * 2 + lax.rem(col, 2)
    y = col // (2 * NZ)
    z = lax.rem(col // 2, NZ)
    root = (y == 0) & (z == 0)
    mate = device(x, y, z, 1 - core)
    x_far = device(wrap(x + 2, NX), y, z, core)

    partners = [mate]
    partners += [device(wrap(x + d, NX), y, z, core) for d in (1, 2, 3)]
    partners += [device(x, wrap(y + d, NY), z, core) for d in (1, 2, 3)]
    partners += [device(x, y, wrap(z + d, NZ), core) for d in (1, -1)]
    barrier = pltpu.get_barrier_semaphore()
    for partner in partners:
        pl.semaphore_signal(barrier, inc=1, device_id=partner, device_id_type=MESH)

    @pl.when(jnp.logical_not(root))
    def _():
        pl.semaphore_signal(barrier, inc=1, device_id=device(x, 0, 0, core), device_id_type=MESH)
        pl.semaphore_wait(barrier, len(partners))

    @pl.when(root)
    def _():
        pl.semaphore_wait(barrier, len(partners) + NY * NZ - 1)

    def run(c):
        def start_row(yy, zz):
            return pl.multiple_of(PIECE * (yy * NZ + zz if c == 0 else zz * NY + yy), PIECE)

        def unit(yy, zz):
            return pan.at[c, :, pl.ds(start_row(yy, zz), PIECE), :]

        def piece(xx, yy, zz):
            return pan.at[c, xx, pl.ds(start_row(yy, zz), PIECE), :]

        def unit_sem(yy, zz):
            return unit_recv.at[yy * NZ + zz]

        @pl.when(root)
        def _():
            def send_piece(i, carry):
                yy = i // NZ
                zz = lax.rem(i, NZ)
                remote(
                    a_ref.at[pl.ds(start_row(yy, zz), PIECE), :], piece(x, yy, zz),
                    s1_send, s1_recv, device(x, yy, zz, c),
                ).start()
                return carry

            lax.fori_loop(1, NY * NZ, send_piece, 0)
            mine = pltpu.make_async_copy(
                a_ref.at[pl.ds(start_row(0, 0), PIECE), :], piece(x, 0, 0), local_sem
            )
            mine.start()
            mine.wait()

        chunk = PW // CHUNKS
        base = row * PW
        far_base = (wrap(xh + 1, 2) * 2 + c) * PW
        for i in range(CHUNKS):
            remote(
                a_ref.at[pl.ds(i * chunk, chunk), :],
                own.at[pl.ds(base + i * chunk, chunk), :],
                e1_send, e1_recv.at[i], x_far,
            ).start()
        remote(a_ref, own.at[pl.ds(base, PW), :], e2_send, e2_recv, mate).start()
        keep = pltpu.make_async_copy(a_ref, own.at[pl.ds(base, PW), :], local_sem)
        keep.start()
        keep.wait()

        def pass_far(i):
            rows = own.at[pl.ds(far_base + i * chunk, chunk), :]
            remote(rows, rows, e1_send, e1_recv.at[i], x_far).wait_recv()
            remote(rows, rows, e3_send, e3_recv, mate).start()

        @pl.when(jnp.logical_not(root))
        def _():
            remote(piece(x, y, z), piece(x, y, z), s1_send, s1_recv, mate).wait_recv()

        for d in (1, 2, 3):
            remote(
                piece(x, y, z), piece(x, y, z), sx_send, sx_recv.at[d - 1],
                device(wrap(x + d, NX), y, z, c),
            ).start()
        for d in (1, 2, 3):
            got = piece(wrap(x - d, NX), y, z)
            remote(got, got, sx_send, sx_recv.at[d - 1], mate).wait_recv()

        def send_z(yy, zz, d):
            remote(
                unit(yy, zz), unit(yy, zz), sz_send, unit_sem(yy, zz), device(x, y, wrap(z + d, NZ), c)
            ).start()

        def send_y(yy, zz):
            for d in (1, 3, 2):
                remote(
                    unit(yy, zz), unit(yy, zz), sy_send, unit_sem(yy, zz),
                    device(x, wrap(y + d, NY), z, c),
                ).start()

        def send_mate(yy, zz):
            remote(unit(yy, zz), unit(yy, zz), swap_send, swap_recv, mate).start()

        def arrived(yy, zz):
            remote(unit(yy, zz), unit(yy, zz), sz_send, unit_sem(yy, zz), mate).wait_recv()

        if c == 0:
            send_z(y, z, 1)
            send_z(y, z, -1)
            send_y(y, z)
            send_mate(y, z)
            late = [z]
            for s in (1, 2, 3, 4):
                now = []
                zz = wrap(z - s, NZ)
                arrived(y, zz)
                if s < 4:
                    send_z(y, zz, 1)
                send_y(y, zz)
                send_mate(y, zz)
                now.append(zz)
                if s < 4:
                    zz = wrap(z + s, NZ)
                    arrived(y, zz)
                    if s < 3:
                        send_z(y, zz, -1)
                    send_y(y, zz)
                    send_mate(y, zz)
                    now.append(zz)
                for zz in late:
                    for d in (1, 3, 2):
                        yy = wrap(y - d, NY)
                        arrived(yy, zz)
                        send_mate(yy, zz)
                late = now
                pass_far(s - 1)
            for zz in late:
                for d in (1, 3, 2):
                    yy = wrap(y - d, NY)
                    arrived(yy, zz)
                    send_mate(yy, zz)
            z_units, y_units = 7, 24
        else:
            send_y(y, z)
            order = [y] + [wrap(y + d, NY) for d in (1, 3, 2)]
            for yy in order:
                if yy is not y:
                    arrived(yy, z)
                send_z(yy, z, 1)
                send_z(yy, z, -1)
                send_mate(yy, z)
            for s in (1, 2, 3, 4):
                for yy in order:
                    zz = wrap(z - s, NZ)
                    arrived(yy, zz)
                    if s < 4:
                        send_z(yy, zz, 1)
                    send_mate(yy, zz)
                    if s < 4:
                        zz = wrap(z + s, NZ)
                        arrived(yy, zz)
                        if s < 3:
                            send_z(yy, zz, -1)
                        send_mate(yy, zz)
                pass_far(s - 1)
            z_units, y_units = 28, 3

        def whole(send, recv, ref):
            return remote(ref, ref, send, recv, mate)

        whole(sz_send, swap_recv, pan.at[c, :, pl.ds(0, PIECE * z_units), :]).wait_send()
        whole(sy_send, swap_recv, pan.at[c, :, pl.ds(0, PIECE * y_units), :]).wait_send()
        whole(sx_send, swap_recv, pan.at[c, pl.ds(0, 3), pl.ds(0, PIECE), :]).wait_send()
        whole(swap_send, swap_recv, pan.at[c]).wait_send()
        whole(swap_send, swap_recv, pan.at[1 - c]).wait_recv()
        block = own.at[pl.ds(0, PW), :]
        whole(e1_send, e3_recv, block).wait_send()
        whole(e2_send, e2_recv, block).wait()
        whole(e3_send, e3_recv, block).wait()

        @pl.when(root)
        def _():
            rest = pan.at[c, 0, pl.ds(0, PIECE * (NY * NZ - 1)), :]
            whole(s1_send, swap_recv, rest).wait_send()

    for c in (0, 1):
        pl.when(core == c)(functools.partial(run, c))

    first = pivots_ref[0:1, :].astype(F32)
    second = pivots_ref[1:2, :].astype(F32)
    src0 = column(first)
    src1 = swapped(column(second), first, 0.0)
    place = lax.broadcasted_iota(jnp.int32, (PW, 1), 0) + row * PW
    srcr = swapped(swapped(place.astype(F32), second, float(PW)), first, 0.0)

    lane = lax.broadcasted_iota(jnp.int32, (PW, PW), 1)

    def one_hot(src, q):
        return jnp.where((lane + q * PW).astype(F32) == src, 1.0, 0.0).astype(BF16)

    def take(src, load, dst):
        dst[...] = jnp.zeros((PW, PW), F32)

        def step(q, carry):
            high, low = split(load(q))
            pick = one_hot(src, q)
            dst[...] += dot(pick, high) + dot(pick, low)
            return carry

        lax.fori_loop(0, 4, step, 0)

    def own_block(q):
        return own[pl.ds(pl.multiple_of(q * PW, PW), PW), :]

    def panel_block(b):
        return lambda q: pan[lax.rem(q, 2), (q // 2) * 2 + b]

    take(src0, own_block, acc_a)

    @pl.when((row == 0) & (col == 0))
    def _():
        o_ref[...] = acc_a[...]

    @pl.when(jnp.logical_not((row == 0) & (col == 0)))
    def _():
        acc_a[...] = dot3(lower_ref[0], acc_a[...])

    @pl.when((row == 0) & (col > 0))
    def _():
        o_ref[...] = acc_a[...]

    @pl.when(row > 0)
    def _():
        take(src1, panel_block(0), acc_b)
        acc_b[...] = dot3(acc_b[...], upper_ref[0])

        @pl.when((row == 1) & (col == 0))
        def _():
            o_ref[...] = acc_b[...]

        @pl.when(jnp.logical_not((row == 1) & (col == 0)))
        def _():
            take(src1, own_block, acc_c)
            acc_c[...] = acc_c[...] - dot3(acc_b[...], acc_a[...])

        @pl.when((row == 1) & (col == 1))
        def _():
            o_ref[...] = acc_c[...]

        @pl.when((row > 1) | (col > 1))
        def _():
            acc_c[...] = dot3(lower_ref[1], acc_c[...])

        @pl.when((row == 1) & (col > 1))
        def _():
            o_ref[...] = acc_c[...]

    @pl.when(row > 1)
    def _():
        take(srcr, panel_block(0), acc_b)
        acc_b[...] = dot3(acc_b[...], upper_ref[0])

        @pl.when(col == 0)
        def _():
            o_ref[...] = acc_b[...]

        @pl.when(col > 0)
        def _():
            take(src0, panel_block(1), acc_d)
            acc_d[...] = dot3(lower_ref[0], acc_d[...])
            o_ref[...] = dot3(acc_b[...], acc_d[...])
            take(srcr, panel_block(1), acc_d)
            acc_d[...] = dot3(acc_d[...] - o_ref[...], upper_ref[1])

        @pl.when(col == 1)
        def _():
            o_ref[...] = acc_d[...]

        @pl.when(col > 1)
        def _():
            take(srcr, own_block, o_ref)
            o_ref[...] = o_ref[...] - dot3(acc_b[...], acc_a[...]) - dot3(acc_d[...], acc_c[...])


def local(matrix, lower_inverses, upper_inverses, pivots):
    vmem = pl.BlockSpec(memory_space=pltpu.VMEM)
    dma = pltpu.SemaphoreType.DMA
    block = pltpu.VMEM((PW, PW), F32)
    return pl.pallas_call(
        kernel,
        out_shape=jax.ShapeDtypeStruct((PW, PW), F32),
        in_specs=[pl.BlockSpec(memory_space=pl.ANY), vmem, vmem, vmem],
        out_specs=vmem,
        scratch_shapes=[
            pltpu.VMEM((2, NX, PW, PW), F32),
            pltpu.VMEM((4 * PW, PW), F32),
            block, block, block, block,
            dma, dma, dma, dma((3,)), dma, dma, dma((NY * NZ,)), dma, dma,
            dma, dma((CHUNKS,)), dma, dma, dma, dma, dma,
        ],
        compiler_params=pltpu.CompilerParams(
            collective_id=0, has_side_effects=True, vmem_limit_bytes=56 * 2**20
        ),
        name="panels",
    )(matrix, lower_inverses, upper_inverses, pivots)


def solution(mesh):
    return jax.shard_map(
        local,
        mesh=mesh,
        in_specs=(P("row", "col"), P(), P(), P()),
        out_specs=P("row", "col"),
        check_vma=False,
    )
```

```python
import functools

import jax
import jax.numpy as jnp
from jax import lax
from jax.experimental import pallas as pl
from jax.experimental.pallas import tpu as pltpu
from jax.sharding import PartitionSpec as P

MESH = pl.DeviceIdType.MESH
PW = 512
NX, NY, NZ = 4, 4, 8
PIECE = 16
CHUNKS = 4
LANES = 128
OWN_0, OWN_1, OWN_R, PANEL_0_1, PANEL_0_R, PANEL_1_0, PANEL_1_R = range(7)
F32 = jnp.float32
BF16 = jnp.bfloat16


def split(value):
    high = value.astype(BF16)
    return high, (value - high.astype(F32)).astype(BF16)


def dot(a, b):
    return jnp.dot(a, b, preferred_element_type=F32)


def dot3(a, b):
    return dot(a[0], b[0]) + (dot(a[0], b[1]) + dot(a[1], b[0]))


def device(x, y, z, core):
    return ((y * NZ + z) * 2 + lax.rem(x, 2), (x // 2) * 2 + core)


def wrap(value, size):
    return lax.rem(value + size, size)


def remote(src, dst, send, recv, target):
    return pltpu.make_async_remote_copy(
        src_ref=src, dst_ref=dst, send_sem=send, recv_sem=recv, device_id=target, device_id_type=MESH
    )


def column(row):
    shape = (PW, PW)
    eye = lax.broadcasted_iota(jnp.int32, shape, 0) == lax.broadcasted_iota(jnp.int32, shape, 1)
    return jnp.sum(jnp.where(eye, row, 0.0), axis=1, keepdims=True)


def swapped(rows, pivot_row, offset):
    lane = lax.broadcasted_iota(jnp.int32, (PW, PW), 1).astype(F32) + offset
    return rows + jnp.sum(jnp.where(pivot_row == rows, lane - rows, 0.0), axis=1, keepdims=True)


def kernel(
    a_ref, lower_ref, upper_ref, pivots_ref, o_ref,
    pan, own, acc, inverses, high_parts, low_parts, src,
    s1_send, s1_recv, sx_send, sx_recv, sz_send, sy_send, unit_recv, swap_send, swap_recv,
    e1_send, e1_recv, e2_send, e2_recv, e3_send, e3_recv, local_sem, keep_sem, inverse_sem,
):
    col = lax.axis_index("col")
    row = lax.axis_index("row")
    core = lax.rem(row, 2)
    xh = row // 2
    x = xh * 2 + lax.rem(col, 2)
    y = col // (2 * NZ)
    z = lax.rem(col // 2, NZ)
    root = (y == 0) & (z == 0)
    mate = device(x, y, z, 1 - core)
    x_far = device(wrap(x + 2, NX), y, z, core)

    partners = [mate]
    partners += [device(wrap(x + d, NX), y, z, core) for d in (1, 2, 3)]
    partners += [device(x, wrap(y + d, NY), z, core) for d in (1, 2, 3)]
    partners += [device(x, y, wrap(z + d, NZ), core) for d in (1, -1)]
    barrier = pltpu.get_barrier_semaphore()
    for partner in partners:
        pl.semaphore_signal(barrier, inc=1, device_id=partner, device_id_type=MESH)

    @pl.when(jnp.logical_not(root))
    def _():
        pl.semaphore_signal(barrier, inc=1, device_id=device(x, 0, 0, core), device_id_type=MESH)

    loads = [
        pltpu.make_async_copy(lower_ref, inverses.at[0], inverse_sem.at[0]),
        pltpu.make_async_copy(upper_ref, inverses.at[1], inverse_sem.at[1]),
    ]
    for load in loads:
        load.start()

    first = pivots_ref[0:1, :].astype(F32)
    second = pivots_ref[1:2, :].astype(F32)
    place = (lax.broadcasted_iota(jnp.int32, (PW, 1), 0) + row * PW).astype(F32)
    src[0] = jnp.broadcast_to(column(first), (PW, LANES))
    src[1] = jnp.broadcast_to(swapped(column(second), first, 0.0), (PW, LANES))
    src[2] = jnp.broadcast_to(swapped(swapped(place, second, float(PW)), first, 0.0), (PW, LANES))
    acc[...] = jnp.zeros(acc.shape, F32)

    @pl.when(jnp.logical_not(root))
    def _():
        pl.semaphore_wait(barrier, len(partners))

    @pl.when(root)
    def _():
        pl.semaphore_wait(barrier, len(partners) + NY * NZ - 1)

    lane = lax.broadcasted_iota(jnp.int32, (1, LANES), 1)

    def take(values, ids, targets):
        high, low = split(values)
        for which, dst in targets:
            pick = jnp.concatenate(
                [jnp.where(src[which] == part.astype(F32), 1.0, 0.0).astype(BF16) for part in ids], axis=1
            )
            acc[dst] += dot(pick, high) + dot(pick, low)

    def own_item(half, i):
        start = half * 2 * PW + i * LANES
        starts = [pl.multiple_of(start + j * PW, LANES) for j in (0, 1)]
        values = jnp.concatenate([own[pl.ds(at, LANES), :] for at in starts], axis=0)
        take(values, [lane + at for at in starts], [(0, OWN_0), (1, OWN_1), (2, OWN_R)])

    def panel_item(zz, b):
        rows = [pl.multiple_of(yy * LANES + zz * PIECE, PIECE) for yy in range(NY)]
        parts = [pan[0, 2 * q + b, pl.ds(at, PIECE), :] for q in (0, 1) for at in rows]
        at = pl.multiple_of(zz * 64, 64)
        parts += [pan[1, 2 * q + b, pl.ds(at, 64), :] for q in (0, 1)]
        within = lax.rem(lane, 64)
        high = (lane // 64) * (2 * PW)
        ids = [
            high + (within // PIECE) * LANES + lax.rem(within, PIECE) + zz * PIECE,
            high + PW + within + zz * 64,
        ]
        targets = [(2, PANEL_0_R), (1, PANEL_0_1)] if b == 0 else [(2, PANEL_1_R), (0, PANEL_1_0)]
        take(jnp.concatenate(parts, axis=0), ids, targets)

    def level(s):
        return [z] if s == 0 else [wrap(z + 4, NZ)] if s == 4 else [wrap(z - s, NZ), wrap(z + s, NZ)]

    def run(c):
        def start_row(yy, zz):
            return pl.multiple_of(PIECE * (yy * NZ + zz if c == 0 else zz * NY + yy), PIECE)

        def unit(yy, zz):
            return pan.at[c, :, pl.ds(start_row(yy, zz), PIECE), :]

        def half_unit(yy, zz, h):
            return pan.at[c, pl.ds(2 * h, 2), pl.ds(start_row(yy, zz), PIECE), :]

        def piece(xx, yy, zz):
            return pan.at[c, xx, pl.ds(start_row(yy, zz), PIECE), :]

        def unit_sem(yy, zz):
            return unit_recv.at[yy * NZ + zz]

        @pl.when(root)
        def _():
            def send_piece(i, carry):
                yy = i // NZ
                zz = lax.rem(i, NZ)
                remote(
                    a_ref.at[pl.ds(start_row(yy, zz), PIECE), :], piece(x, yy, zz),
                    s1_send, s1_recv, device(x, yy, zz, c),
                ).start()
                return carry

            lax.fori_loop(1, NY * NZ, send_piece, 0)
            mine = pltpu.make_async_copy(
                a_ref.at[pl.ds(start_row(0, 0), PIECE), :], piece(x, 0, 0), local_sem
            )
            mine.start()
            mine.wait()

        chunk = PW // CHUNKS
        base = row * PW
        far_base = (wrap(xh + 1, 2) * 2 + c) * PW

        def send_far(i):
            remote(
                a_ref.at[pl.ds(i * chunk, chunk), :],
                own.at[pl.ds(base + i * chunk, chunk), :],
                e1_send, e1_recv.at[i], x_far,
            ).start()

        def pass_far(i):
            rows = own.at[pl.ds(far_base + i * chunk, chunk), :]
            remote(rows, rows, e1_send, e1_recv.at[i], x_far).wait_recv()
            remote(rows, rows, e3_send, e3_recv.at[i], mate).start()

        def far_item(i):
            rows = own.at[pl.ds((wrap(xh + 1, 2) * 2 + 1 - c) * PW + i * chunk, chunk), :]
            remote(rows, rows, e3_send, e3_recv.at[i], mate).wait_recv()
            own_item(wrap(xh + 1, 2), i)

        send_far(0)
        near = remote(a_ref, own.at[pl.ds(base, PW), :], e2_send, e2_recv, mate)
        near.start()
        keep = pltpu.make_async_copy(a_ref, own.at[pl.ds(base, PW), :], keep_sem)
        keep.start()
        keep.wait()
        near.wait()
        for i in range(CHUNKS):
            own_item(xh, i)

        @pl.when(jnp.logical_not(root))
        def _():
            remote(piece(x, y, z), piece(x, y, z), s1_send, s1_recv, mate).wait_recv()

        for d in (1, 3, 2):
            remote(
                piece(x, y, z), piece(x, y, z), sx_send, sx_recv.at[d - 1],
                device(wrap(x + d, NX), y, z, c),
            ).start()
        for i in range(1, CHUNKS):
            send_far(i)
        pass_far(0)
        for d in (1, 3, 2):
            got = piece(wrap(x - d, NX), y, z)
            remote(got, got, sx_send, sx_recv.at[d - 1], mate).wait_recv()

        def send_z(yy, zz, d):
            remote(
                unit(yy, zz), unit(yy, zz), sz_send, unit_sem(yy, zz), device(x, y, wrap(z + d, NZ), c)
            ).start()

        def send_y(ref, yy, zz, d):
            remote(ref, ref, sy_send, unit_sem(yy, zz), device(x, wrap(y + d, NY), z, c)).start()

        def send_mate(yy, zz, s):
            remote(unit(yy, zz), unit(yy, zz), swap_send, swap_recv.at[s], mate).start()

        def arrived(yy, zz):
            remote(unit(yy, zz), unit(yy, zz), sz_send, unit_sem(yy, zz), mate).wait_recv()

        def swapped_in(s):
            ref = pan.at[1 - c, :, pl.ds(0, 64 * len(level(s))), :]
            remote(ref, ref, swap_send, swap_recv.at[s], mate).wait_recv()

        def items(s):
            return [functools.partial(panel_item, zz, b) for zz in level(s) for b in (0, 1)]

        if c == 0:
            def both_ways(zz, s):
                send_y(unit(y, zz), y, zz, 1)
                send_y(unit(y, zz), y, zz, -1)
                send_mate(y, zz, s)

            send_z(y, z, 1)
            send_z(y, z, -1)
            both_ways(z, 0)
            for s in range(1, 7):
                work = []
                if s >= 3:
                    swapped_in(s - 3)
                    work = items(s - 3)
                if s <= 4:
                    zz = wrap(z - s, NZ)
                    arrived(y, zz)
                    if s < 4:
                        send_z(y, zz, 1)
                    both_ways(zz, s)
                if s < 4:
                    zz = wrap(z + s, NZ)
                    arrived(y, zz)
                    if s < 3:
                        send_z(y, zz, -1)
                    both_ways(zz, s)
                for item in work[:1]:
                    item()
                if s - 1 <= 4:
                    for zz in level(s - 1):
                        yy = wrap(y - 1, NY)
                        arrived(yy, zz)
                        send_y(half_unit(yy, zz, 0), yy, zz, 1)
                        send_mate(yy, zz, s - 1)
                        yy = wrap(y + 1, NY)
                        arrived(yy, zz)
                        send_y(half_unit(yy, zz, 1), yy, zz, -1)
                        send_mate(yy, zz, s - 1)
                for item in work[1:3]:
                    item()
                if s >= 2:
                    for zz in level(s - 2):
                        yy = wrap(y + 2, NY)
                        arrived(yy, zz)
                        send_mate(yy, zz, s - 2)
                for item in work[3:]:
                    item()
                if s == 1:
                    far_item(0)
                if s in (2, 3, 4):
                    pass_far(s - 1)
                if s in (3, 4, 5):
                    far_item(s - 2)
            z_units, y_units = 7, 24
        else:
            for d in (1, 3, 2):
                send_y(unit(y, z), y, z, d)
            order = [y] + [wrap(y + d, NY) for d in (1, 3, 2)]
            for yy in order:
                if yy is not y:
                    arrived(yy, z)
                send_z(yy, z, 1)
                send_z(yy, z, -1)
                send_mate(yy, z, 0)
            for s in (1, 2, 3, 4):
                work = []
                if s >= 2:
                    work = items(s - 2)
                for k, yy in enumerate(order):
                    if s < 4 or k < 2:
                        zz = wrap(z - s, NZ)
                        arrived(yy, zz)
                        if s < 3 or (s == 3 and k < 2):
                            send_z(yy, zz, 1)
                        send_mate(yy, zz, s)
                    if s < 4 or k >= 2:
                        zz = wrap(z + s, NZ)
                        arrived(yy, zz)
                        if s < 3 or (s == 3 and k >= 2):
                            send_z(yy, zz, -1)
                        send_mate(yy, zz, s)
                    if k == 0 and work:
                        swapped_in(s - 2)
                    for item in work[k:k + 1]:
                        item()
                if s == 1:
                    far_item(0)
                if s in (2, 3, 4):
                    pass_far(s - 1)
                if s in (3, 4):
                    far_item(s - 2)
            swapped_in(3)
            for item in items(3):
                item()
            far_item(3)
            z_units, y_units = 28, 3

        def whole(send, recv, ref):
            return remote(ref, ref, send, recv, mate)

        swapped_in(4)
        block = own.at[pl.ds(0, PW), :]
        whole(sz_send, s1_recv, pan.at[c, :, pl.ds(0, PIECE * z_units), :]).wait_send()
        whole(sy_send, s1_recv, pan.at[c, :, pl.ds(0, PIECE * y_units), :]).wait_send()
        whole(sx_send, s1_recv, pan.at[c, pl.ds(0, 3), pl.ds(0, PIECE), :]).wait_send()
        whole(swap_send, s1_recv, pan.at[c]).wait_send()
        whole(e1_send, s1_recv, block).wait_send()
        whole(e3_send, s1_recv, block).wait_send()

        @pl.when(root)
        def _():
            rest = pan.at[c, 0, pl.ds(0, PIECE * (NY * NZ - 1)), :]
            whole(s1_send, s1_recv, rest).wait_send()

    for load in loads:
        load.wait()
    for i in range(4):
        high_parts[i], low_parts[i] = split(inverses[i // 2, i % 2])

    def inverse(i):
        return high_parts[i], low_parts[i]

    lower0, lower1, upper0, upper1 = [functools.partial(inverse, i) for i in range(4)]

    for c in (0, 1):
        pl.when(core == c)(functools.partial(run, c))

    for b in (0, 1):
        panel_item(level(4)[0], b)

    def put(condition, value):
        @pl.when(condition)
        def _():
            o_ref[...] = value

    put((row == 0) & (col == 0), acc[OWN_0])
    upper_rows = dot3(lower0(), split(acc[OWN_0]))
    put((row == 0) & (col > 0), upper_rows)
    top = split(upper_rows)
    lower_cols = dot3(split(acc[PANEL_0_1]), upper0())
    put((row == 1) & (col == 0), lower_cols)
    middle = acc[OWN_1] - dot3(split(lower_cols), top)
    put((row == 1) & (col == 1), middle)
    middle = dot3(lower1(), split(middle))
    put((row == 1) & (col > 1), middle)
    lower_cols = dot3(split(acc[PANEL_0_R]), upper0())
    put((row > 1) & (col == 0), lower_cols)
    lower_cols = split(lower_cols)
    rest = acc[OWN_R] - dot3(lower_cols, top)
    panel_top = dot3(lower0(), split(acc[PANEL_1_0]))
    lower_cols = acc[PANEL_1_R] - dot3(lower_cols, split(panel_top))
    lower_cols = dot3(split(lower_cols), upper1())
    put((row > 1) & (col == 1), lower_cols)
    put((row > 1) & (col > 1), rest - dot3(split(lower_cols), split(middle)))


def local(matrix, lower_inverses, upper_inverses, pivots):
    vmem = pl.BlockSpec(memory_space=pltpu.VMEM)
    dma = pltpu.SemaphoreType.DMA
    anywhere = pl.BlockSpec(memory_space=pl.ANY)
    return pl.pallas_call(
        kernel,
        out_shape=jax.ShapeDtypeStruct((PW, PW), F32),
        in_specs=[anywhere, anywhere, anywhere, vmem],
        out_specs=vmem,
        scratch_shapes=[
            pltpu.VMEM((2, NX, PW, PW), F32),
            pltpu.VMEM((4 * PW, PW), F32),
            pltpu.VMEM((7, PW, PW), F32),
            pltpu.VMEM((2, 2, PW, PW), F32),
            pltpu.VMEM((4, PW, PW), BF16),
            pltpu.VMEM((4, PW, PW), BF16),
            pltpu.VMEM((3, PW, LANES), F32),
            dma, dma, dma, dma((3,)), dma, dma, dma((NY * NZ,)), dma, dma((5,)),
            dma, dma((CHUNKS,)), dma, dma, dma, dma((CHUNKS,)), dma, dma, dma((2,)),
        ],
        compiler_params=pltpu.CompilerParams(
            collective_id=0, has_side_effects=True, vmem_limit_bytes=56 * 2**20
        ),
        name="panels",
    )(matrix, lower_inverses, upper_inverses, pivots)


def solution(mesh):
    return jax.shard_map(
        local,
        mesh=mesh,
        in_specs=(P("row", "col"), P(), P(), P()),
        out_specs=P("row", "col"),
        check_vma=False,
    )
```

```python
import functools

import jax
import jax.numpy as jnp
from jax import lax
from jax.experimental import pallas as pl
from jax.experimental.pallas import tpu as pltpu
from jax.sharding import PartitionSpec as P

MESH = pl.DeviceIdType.MESH
PW = 512
NX, NY, NZ = 4, 4, 8
PIECE = 16
CHUNKS = 4
LANES = 128
LAG_1, LAG = 2, 4
OWN_0, OWN_1, OWN_R, PANEL_0_1, PANEL_0_R, PANEL_1_0, PANEL_1_R = range(7)
F32 = jnp.float32
BF16 = jnp.bfloat16


def split(value):
    high = value.astype(BF16)
    return high, (value - high.astype(F32)).astype(BF16)


def dot(a, b):
    return jnp.dot(a, b, preferred_element_type=F32)


def dot3(a, b):
    return dot(jnp.concatenate([a[0], a[0], a[1]], axis=1), jnp.concatenate([b[0], b[1], b[0]], axis=0))


def dot3_upper(a, b):
    h = PW // 2
    left = dot3([part[:, :h] for part in a], [part[:h, :h] for part in b])
    right = dot3(a, [part[:, h:] for part in b])
    return jnp.concatenate([left, right], axis=1)


def dot3_lower(a, b):
    h = PW // 2
    above = dot3([part[:h, :h] for part in a], [part[:h, :] for part in b])
    below = dot3([part[h:, :] for part in a], b)
    return jnp.concatenate([above, below], axis=0)


def device(x, y, z, core):
    return ((y * NZ + z) * 2 + lax.rem(x, 2), (x // 2) * 2 + core)


def wrap(value, size):
    return lax.rem(value + size, size)


def remote(src, dst, send, recv, target):
    return pltpu.make_async_remote_copy(
        src_ref=src, dst_ref=dst, send_sem=send, recv_sem=recv, device_id=target, device_id_type=MESH
    )


def column(row):
    shape = (PW, PW)
    eye = lax.broadcasted_iota(jnp.int32, shape, 0) == lax.broadcasted_iota(jnp.int32, shape, 1)
    return jnp.sum(jnp.where(eye, row, 0.0), axis=1, keepdims=True)


def swapped(rows, pivot_row, offset):
    lane = lax.broadcasted_iota(jnp.int32, (PW, PW), 1).astype(F32) + offset
    return rows + jnp.sum(jnp.where(pivot_row == rows, lane - rows, 0.0), axis=1, keepdims=True)


def kernel(
    a_ref, lower_ref, upper_ref, pivots_ref, o_ref,
    pan, own, acc, inverses, high_parts, low_parts, src,
    s1_send, s1_recv, sx_send, sx_recv, sz_send, sy_send, unit_recv, swap_send, swap_recv,
    e1_send, e1_recv, e2_send, e2_recv, e3_send, e3_recv, local_sem, keep_sem, inverse_sem,
):
    col = lax.axis_index("col")
    row = lax.axis_index("row")
    core = lax.rem(row, 2)
    xh = row // 2
    x = xh * 2 + lax.rem(col, 2)
    y = col // (2 * NZ)
    z = lax.rem(col // 2, NZ)
    root = (y == 0) & (z == 0)
    mate = device(x, y, z, 1 - core)
    x_far = device(wrap(x + 2, NX), y, z, core)

    partners = [mate]
    partners += [device(wrap(x + d, NX), y, z, core) for d in (1, 2, 3)]
    partners += [device(x, wrap(y + d, NY), z, core) for d in (1, 2, 3)]
    partners += [device(x, y, wrap(z + d, NZ), core) for d in (1, -1)]
    barrier = pltpu.get_barrier_semaphore()
    for partner in partners:
        pl.semaphore_signal(barrier, inc=1, device_id=partner, device_id_type=MESH)

    @pl.when(jnp.logical_not(root))
    def _():
        pl.semaphore_signal(barrier, inc=1, device_id=device(x, 0, 0, core), device_id_type=MESH)

    loads = [
        pltpu.make_async_copy(lower_ref, inverses.at[0], inverse_sem.at[0]),
        pltpu.make_async_copy(upper_ref, inverses.at[1], inverse_sem.at[1]),
    ]
    for load in loads:
        load.start()

    first = pivots_ref[0:1, :].astype(F32)
    second = pivots_ref[1:2, :].astype(F32)
    place = (lax.broadcasted_iota(jnp.int32, (PW, 1), 0) + row * PW).astype(F32)
    src[0] = jnp.broadcast_to(column(first), (PW, LANES))
    src[1] = jnp.broadcast_to(swapped(column(second), first, 0.0), (PW, LANES))
    src[2] = jnp.broadcast_to(swapped(swapped(place, second, float(PW)), first, 0.0), (PW, LANES))
    acc[...] = jnp.zeros(acc.shape, F32)

    @pl.when(jnp.logical_not(root))
    def _():
        pl.semaphore_wait(barrier, len(partners))

    @pl.when(root)
    def _():
        pl.semaphore_wait(barrier, len(partners) + NY * NZ - 1)

    def inverse(i):
        return high_parts[i], low_parts[i]

    lower0, lower1, upper0, upper1, top = [functools.partial(inverse, i) for i in range(5)]

    def put(condition, value):
        @pl.when(condition)
        def _():
            o_ref[...] = value

    def solve_top():
        value = dot3_lower(lower0(), split(acc[OWN_0]))
        put((row == 0) & (col == 0), acc[OWN_0])
        put((row == 0) & (col > 0), value)
        high_parts[4], low_parts[4] = split(value)

    lane = lax.broadcasted_iota(jnp.int32, (1, LANES), 1)

    def take(values, ids, targets):
        high, low = split(values)
        for which, dst in targets:
            pick = jnp.concatenate(
                [jnp.where(src[which] == part.astype(F32), 1.0, 0.0).astype(BF16) for part in ids], axis=1
            )
            acc[dst] += dot(jnp.concatenate([pick, pick], axis=1), jnp.concatenate([high, low], axis=0))

    def own_item(half, i):
        start = half * 2 * PW + i * LANES
        starts = [pl.multiple_of(start + j * PW, LANES) for j in (0, 1)]
        values = jnp.concatenate([own[pl.ds(at, LANES), :] for at in starts], axis=0)
        take(values, [lane + at for at in starts], [(0, OWN_0), (1, OWN_1), (2, OWN_R)])

    def panel_item(zz, b):
        rows = [pl.multiple_of(yy * LANES + zz * PIECE, PIECE) for yy in range(NY)]
        parts = [pan[0, 2 * q + b, pl.ds(at, PIECE), :] for q in (0, 1) for at in rows]
        at = pl.multiple_of(zz * 64, 64)
        parts += [pan[1, 2 * q + b, pl.ds(at, 64), :] for q in (0, 1)]
        within = lax.rem(lane, 64)
        high = (lane // 64) * (2 * PW)
        ids = [
            high + (within // PIECE) * LANES + lax.rem(within, PIECE) + zz * PIECE,
            high + PW + within + zz * 64,
        ]
        targets = [(2, PANEL_0_R), (1, PANEL_0_1)] if b == 0 else [(2, PANEL_1_R), (0, PANEL_1_0)]
        values = jnp.concatenate(parts, axis=0)
        if b == 0:
            values = dot3_upper(split(values), upper0())
        take(values, ids, targets)

    def nth(j):
        return wrap(z + (1 - 2 * lax.rem(j, 2)) * ((j + 1) // 2), NZ)

    def start_row(yy, zz, c):
        return pl.multiple_of(PIECE * ((yy * NZ + zz) * (1 - c) + (zz * NY + yy) * c), PIECE)

    def unit(yy, zz, c):
        return pan.at[c, :, pl.ds(start_row(yy, zz, c), PIECE), :]

    def half_unit(yy, zz, h, c):
        return pan.at[c, pl.ds(2 * h, 2), pl.ds(start_row(yy, zz, c), PIECE), :]

    def piece(xx, yy, zz):
        return pan.at[core, xx, pl.ds(start_row(yy, zz, core), PIECE), :]

    def unit_sem(yy, zz):
        return unit_recv.at[yy * NZ + zz]

    @pl.when(root)
    def _():
        def send_piece(i, carry):
            yy = lax.rem(i, NY)
            zz = lax.rem(i // NY + 2 * yy, NZ)
            remote(
                a_ref.at[pl.ds(start_row(yy, zz, core), PIECE), :], piece(x, yy, zz),
                s1_send, s1_recv, device(x, yy, zz, core),
            ).start()
            return carry

        lax.fori_loop(1, NY * NZ, send_piece, 0)
        mine = pltpu.make_async_copy(
            a_ref.at[pl.ds(start_row(0, 0, core), PIECE), :], piece(x, 0, 0), local_sem
        )
        mine.start()
        mine.wait()

    chunk = PW // CHUNKS
    base = row * PW
    other = wrap(xh + 1, 2)

    def far_rows(c, i):
        return own.at[pl.ds(pl.multiple_of((other * 2 + c) * PW + i * chunk, chunk), chunk), :]

    def send_far(i):
        remote(
            a_ref.at[pl.ds(pl.multiple_of(i * chunk, chunk), chunk), :],
            own.at[pl.ds(pl.multiple_of(base + i * chunk, chunk), chunk), :],
            e1_send, e1_recv.at[i], x_far,
        ).start()

    def pass_far(i):
        rows = far_rows(core, i)
        remote(rows, rows, e1_send, e1_recv.at[i], x_far).wait_recv()
        remote(rows, rows, e3_send, e3_recv.at[i], mate).start()

    def far_item(i):
        rows = far_rows(1 - core, i)
        remote(rows, rows, e3_send, e3_recv.at[i], mate).wait_recv()
        own_item(other, i)

    send_far(0)
    near = remote(a_ref, own.at[pl.ds(base, PW), :], e2_send, e2_recv, mate)
    near.start()
    keep = pltpu.make_async_copy(a_ref, own.at[pl.ds(base, PW), :], keep_sem)
    keep.start()
    for load in loads:
        load.wait()
    for i in range(4):
        high_parts[i], low_parts[i] = split(inverses[i // 2, i % 2])
    keep.wait()
    near.wait()

    def near_item(i, carry):
        own_item(xh, i)
        return carry

    lax.fori_loop(0, CHUNKS, near_item, 0)

    @pl.when(jnp.logical_not(root))
    def _():
        remote(piece(x, y, z), piece(x, y, z), s1_send, s1_recv, mate).wait_recv()

    for d in (1, 3, 2):
        remote(
            piece(x, y, z), piece(x, y, z), sx_send, sx_recv.at[d - 1],
            device(wrap(x + d, NX), y, z, core),
        ).start()
    send_far(1)
    pass_far(0)
    for d in (1, 3, 2):
        got = piece(wrap(x - d, NX), y, z)
        remote(got, got, sx_send, sx_recv.at[d - 1], mate).wait_recv()

    def send_z(yy, zz, d, c):
        ref = unit(yy, zz, c)
        remote(ref, ref, sz_send, unit_sem(yy, zz), device(x, y, wrap(z + d, NZ), c)).start()

    def send_y(ref, yy, zz, d, c):
        remote(ref, ref, sy_send, unit_sem(yy, zz), device(x, wrap(y + d, NY), z, c)).start()

    def send_mate(yy, zz, j, c):
        ref = unit(yy, zz, c)
        remote(ref, ref, swap_send, swap_recv.at[j], mate).start()

    def arrived(yy, zz, c):
        ref = unit(yy, zz, c)
        remote(ref, ref, sz_send, unit_sem(yy, zz), mate).wait_recv()

    def both_ways(zz, j):
        send_y(unit(y, zz, 0), y, zz, 1, 0)
        send_y(unit(y, zz, 0), y, zz, -1, 0)
        send_mate(y, zz, j, 0)

    order = [(0, y)] + [(k + 1, wrap(y + d, NY)) for k, d in enumerate((1, 3, 2))]

    @pl.when(core == 0)
    def _():
        send_z(y, z, 1, 0)
        send_z(y, z, -1, 0)
        both_ways(z, 0)

    @pl.when(core == 1)
    def _():
        for d in (1, 3, 2):
            send_y(unit(y, z, 1), y, z, d, 1)
        for k, yy in order:
            if k > 0:
                arrived(yy, z, 1)
            send_z(yy, z, 1, 1)
            send_z(yy, z, -1, 1)
            send_mate(yy, z, 0, 1)

    def slot_core_0(t):
        @pl.when(t <= 7)
        def _():
            zz = nth(t)
            arrived(y, zz, 0)

            @pl.when((lax.rem(t, 2) == 1) & (t < 7))
            def _():
                send_z(y, zz, 1, 0)

            @pl.when((lax.rem(t, 2) == 0) & (t < 6))
            def _():
                send_z(y, zz, -1, 0)

            both_ways(zz, t)

        @pl.when((t >= LAG_1) & (t <= 7 + LAG_1))
        def _():
            zz = nth(t - LAG_1)
            yy = wrap(y - 1, NY)
            arrived(yy, zz, 0)
            send_y(half_unit(yy, zz, 0, 0), yy, zz, 1, 0)
            send_mate(yy, zz, t - LAG_1, 0)
            yy = wrap(y + 1, NY)
            arrived(yy, zz, 0)
            send_y(half_unit(yy, zz, 1, 0), yy, zz, -1, 0)
            send_mate(yy, zz, t - LAG_1, 0)

        @pl.when(t >= LAG)
        def _():
            zz = nth(t - LAG)
            yy = wrap(y + 2, NY)
            arrived(yy, zz, 0)
            send_mate(yy, zz, t - LAG, 0)

    def slot_core_1(t):
        zz = nth(t)
        up = lax.rem(t, 2) == 1
        for k, yy in order:
            arrived(yy, zz, 1)
            send_mate(yy, zz, t, 1)

            @pl.when(up & ((t < 5) | ((t == 5) & (k < 2))))
            def _():
                send_z(yy, zz, 1, 1)

            @pl.when(jnp.logical_not(up) & ((t < 6) | ((t == 6) & (k >= 2))))
            def _():
                send_z(yy, zz, -1, 1)

    def slot(t, carry):
        @pl.when(core == 0)
        def _():
            slot_core_0(t)

        @pl.when((core == 1) & (t <= 6))
        def _():
            slot_core_1(t)

        @pl.when((t == 2) | (t == 4))
        def _():
            send_far(t // 2 + 1)

        @pl.when((t == 5) | (t == 7) | (t == 9))
        def _():
            pass_far((t - 3) // 2)

        @pl.when(t == 11)
        def _():
            solve_top()

        @pl.when(t >= LAG)
        def _():
            j = t - LAG
            ref = pan.at[1 - core, :, pl.ds(0, 64), :]
            remote(ref, ref, swap_send, swap_recv.at[j], mate).wait_recv()
            for b in (0, 1):
                panel_item(nth(j), b)

        @pl.when((core == 1) & (t == 9))
        def _():
            slot_core_1(7)

        @pl.when((t == 4) | (t == 6) | (t == 8) | (t == 10))
        def _():
            far_item(t // 2 - 2)

        return carry

    lax.fori_loop(1, 8 + LAG, slot, 0)

    put((row == 1) & (col == 0), acc[PANEL_0_1])
    put((row > 1) & (col == 0), acc[PANEL_0_R])
    middle = acc[OWN_1] - dot3(split(acc[PANEL_0_1]), top())
    put((row == 1) & (col == 1), middle)
    middle = dot3_lower(lower1(), split(middle))
    put((row == 1) & (col > 1), middle)
    lower_cols = split(acc[PANEL_0_R])
    rest = acc[OWN_R] - dot3(lower_cols, top())
    panel_top = dot3_lower(lower0(), split(acc[PANEL_1_0]))
    lower_cols = acc[PANEL_1_R] - dot3(lower_cols, split(panel_top))
    lower_cols = dot3_upper(split(lower_cols), upper1())
    put((row > 1) & (col == 1), lower_cols)
    put((row > 1) & (col > 1), rest - dot3(split(lower_cols), split(middle)))

    def sent(sem, ref):
        remote(ref, ref, sem, s1_recv, mate).wait_send()

    block = own.at[pl.ds(0, PW), :]
    sent(sx_send, pan.at[0, pl.ds(0, 3), pl.ds(0, PIECE), :])
    sent(swap_send, pan.at[0])
    sent(e1_send, block)
    sent(e3_send, block)

    @pl.when(core == 0)
    def _():
        sent(sz_send, pan.at[0, :, pl.ds(0, PIECE * 7), :])
        sent(sy_send, pan.at[0, :, pl.ds(0, PIECE * 24), :])

    @pl.when(core == 1)
    def _():
        sent(sz_send, pan.at[1, :, pl.ds(0, PIECE * 28), :])
        sent(sy_send, pan.at[1, :, pl.ds(0, PIECE * 3), :])

    @pl.when(root)
    def _():
        sent(s1_send, pan.at[0, 0, pl.ds(0, PIECE * (NY * NZ - 1)), :])


def local(matrix, lower_inverses, upper_inverses, pivots):
    vmem = pl.BlockSpec(memory_space=pltpu.VMEM)
    dma = pltpu.SemaphoreType.DMA
    anywhere = pl.BlockSpec(memory_space=pl.ANY)
    return pl.pallas_call(
        kernel,
        out_shape=pltpu.VMEM((PW, PW), F32),
        in_specs=[anywhere, anywhere, anywhere, vmem],
        out_specs=vmem,
        scratch_shapes=[
            pltpu.VMEM((2, NX, PW, PW), F32),
            pltpu.VMEM((4 * PW, PW), F32),
            pltpu.VMEM((7, PW, PW), F32),
            pltpu.VMEM((2, 2, PW, PW), F32),
            pltpu.VMEM((5, PW, PW), BF16),
            pltpu.VMEM((5, PW, PW), BF16),
            pltpu.VMEM((3, PW, LANES), F32),
            dma, dma, dma, dma((3,)), dma, dma, dma((NY * NZ,)), dma, dma((NZ,)),
            dma, dma((CHUNKS,)), dma, dma, dma, dma((CHUNKS,)), dma, dma, dma((2,)),
        ],
        compiler_params=pltpu.CompilerParams(
            collective_id=0, has_side_effects=True, vmem_limit_bytes=56 * 2**20
        ),
        name="panels",
    )(matrix, lower_inverses, upper_inverses, pivots)


def solution(mesh):
    return jax.shard_map(
        local,
        mesh=mesh,
        in_specs=(P("row", "col"), P(), P(), P()),
        out_specs=P("row", "col"),
        check_vma=False,
    )
```

```python
import functools

import jax
import jax.numpy as jnp
from jax import lax
from jax.experimental import pallas as pl
from jax.experimental.pallas import tpu as pltpu
from jax.sharding import PartitionSpec as P

MESH = pl.DeviceIdType.MESH
PW = 512
NX, NY, NZ = 4, 4, 8
PIECE = 16
CHUNKS = 4
LANES = 128
LAG_1, LAG = 2, 4
OWN_0, OWN_1, OWN_R, PANEL_0_1, PANEL_0_R, PANEL_1_0, PANEL_1_R = range(7)
F32 = jnp.float32
BF16 = jnp.bfloat16


def split(value):
    high = value.astype(BF16)
    return high, (value - high.astype(F32)).astype(BF16)


def dot(a, b):
    return jnp.dot(a, b, preferred_element_type=F32)


def dot3(a, b):
    return dot(jnp.concatenate([a[0], a[0], a[1]], axis=1), jnp.concatenate([b[0], b[1], b[0]], axis=0))


def dot3_upper(a, b):
    h = PW // 2
    left = dot3([part[:, :h] for part in a], [part[:h, :h] for part in b])
    right = dot3(a, [part[:, h:] for part in b])
    return jnp.concatenate([left, right], axis=1)


def dot3_lower(a, b):
    h = PW // 2
    above = dot3([part[:h, :h] for part in a], [part[:h, :] for part in b])
    below = dot3([part[h:, :] for part in a], b)
    return jnp.concatenate([above, below], axis=0)


def device(x, y, z, core):
    return ((y * NZ + z) * 2 + lax.rem(x, 2), (x // 2) * 2 + core)


def wrap(value, size):
    return lax.rem(value + size, size)


def remote(src, dst, send, recv, target):
    return pltpu.make_async_remote_copy(
        src_ref=src, dst_ref=dst, send_sem=send, recv_sem=recv, device_id=target, device_id_type=MESH
    )


def column(row):
    shape = (PW, PW)
    eye = lax.broadcasted_iota(jnp.int32, shape, 0) == lax.broadcasted_iota(jnp.int32, shape, 1)
    return jnp.sum(jnp.where(eye, row, 0.0), axis=1, keepdims=True)


def swapped(rows, pivot_row, offset):
    lane = lax.broadcasted_iota(jnp.int32, (PW, PW), 1).astype(F32) + offset
    return rows + jnp.sum(jnp.where(pivot_row == rows, lane - rows, 0.0), axis=1, keepdims=True)


def kernel(
    a_ref, lower_ref, upper_ref, pivots_ref, o_ref,
    pan, own, acc, inverses, high_parts, low_parts, src,
    s1_send, s1_recv, sx_send, sx_recv, sz_send, sy_send, unit_recv, swap_send, swap_recv,
    e1_send, e1_recv, e2_send, e2_recv, e3_send, e3_recv, local_sem, keep_sem, inverse_sem,
):
    col = lax.axis_index("col")
    row = lax.axis_index("row")
    core = lax.rem(row, 2)
    xh = row // 2
    x = xh * 2 + lax.rem(col, 2)
    y = col // (2 * NZ)
    z = lax.rem(col // 2, NZ)
    root = (y == 0) & (z == 0)
    mate = device(x, y, z, 1 - core)
    x_far = device(wrap(x + 2, NX), y, z, core)

    partners = [mate]
    partners += [device(wrap(x + d, NX), y, z, core) for d in (1, 2, 3)]
    partners += [device(x, wrap(y + d, NY), z, core) for d in (1, 2, 3)]
    partners += [device(x, y, wrap(z + d, NZ), core) for d in (1, -1)]
    barrier = pltpu.get_barrier_semaphore()
    for partner in partners:
        pl.semaphore_signal(barrier, inc=1, device_id=partner, device_id_type=MESH)

    @pl.when(jnp.logical_not(root))
    def _():
        pl.semaphore_signal(barrier, inc=1, device_id=device(x, 0, 0, core), device_id_type=MESH)

    loads = [
        pltpu.make_async_copy(lower_ref, inverses.at[0], inverse_sem.at[0]),
        pltpu.make_async_copy(upper_ref, inverses.at[1], inverse_sem.at[1]),
    ]
    for load in loads:
        load.start()

    first = pivots_ref[0:1, :].astype(F32)
    second = pivots_ref[1:2, :].astype(F32)
    place = (lax.broadcasted_iota(jnp.int32, (PW, 1), 0) + row * PW).astype(F32)
    src[0] = jnp.broadcast_to(column(first), (PW, LANES))
    src[1] = jnp.broadcast_to(swapped(column(second), first, 0.0), (PW, LANES))
    src[2] = jnp.broadcast_to(swapped(swapped(place, second, float(PW)), first, 0.0), (PW, LANES))
    acc[...] = jnp.zeros(acc.shape, F32)

    @pl.when(jnp.logical_not(root))
    def _():
        pl.semaphore_wait(barrier, len(partners))

    @pl.when(root)
    def _():
        pl.semaphore_wait(barrier, len(partners) + NY * NZ - 1)

    def inverse(i):
        return high_parts[i], low_parts[i]

    lower0, lower1, upper0, upper1, top = [functools.partial(inverse, i) for i in range(5)]

    def put(condition, value):
        @pl.when(condition)
        def _():
            o_ref[...] = value

    def solve_top():
        value = dot3_lower(lower0(), split(acc[OWN_0]))
        put((row == 0) & (col == 0), acc[OWN_0])
        put((row == 0) & (col > 0), value)
        high_parts[4], low_parts[4] = split(value)

    lane = lax.broadcasted_iota(jnp.int32, (1, LANES), 1)

    def take(values, ids, targets):
        high, low = split(values)
        for which, dst in targets:
            pick = jnp.concatenate(
                [jnp.where(src[which] == part.astype(F32), 1.0, 0.0).astype(BF16) for part in ids], axis=1
            )
            acc[dst] += dot(jnp.concatenate([pick, pick], axis=1), jnp.concatenate([high, low], axis=0))

    def own_item(half, i):
        start = half * 2 * PW + i * LANES
        starts = [pl.multiple_of(start + j * PW, LANES) for j in (0, 1)]
        values = jnp.concatenate([own[pl.ds(at, LANES), :] for at in starts], axis=0)
        take(values, [lane + at for at in starts], [(0, OWN_0), (1, OWN_1), (2, OWN_R)])

    def panel_item(zz, b):
        rows = [pl.multiple_of(yy * LANES + zz * PIECE, PIECE) for yy in range(NY)]
        parts = [pan[0, 2 * q + b, pl.ds(at, PIECE), :] for q in (0, 1) for at in rows]
        at = pl.multiple_of(zz * 64, 64)
        parts += [pan[1, 2 * q + b, pl.ds(at, 64), :] for q in (0, 1)]
        within = lax.rem(lane, 64)
        high = (lane // 64) * (2 * PW)
        ids = [
            high + (within // PIECE) * LANES + lax.rem(within, PIECE) + zz * PIECE,
            high + PW + within + zz * 64,
        ]
        targets = [(2, PANEL_0_R), (1, PANEL_0_1)] if b == 0 else [(2, PANEL_1_R), (0, PANEL_1_0)]
        values = jnp.concatenate(parts, axis=0)
        if b == 0:
            values = dot3_upper(split(values), upper0())
        take(values, ids, targets)

    def nth(j):
        return wrap(z + (1 - 2 * lax.rem(j, 2)) * ((j + 1) // 2), NZ)

    def start_row(yy, zz, c):
        return pl.multiple_of(PIECE * ((yy * NZ + zz) * (1 - c) + (zz * NY + yy) * c), PIECE)

    def unit(yy, zz, c):
        return pan.at[c, :, pl.ds(start_row(yy, zz, c), PIECE), :]

    def half_unit(yy, zz, h, c):
        return pan.at[c, pl.ds(2 * h, 2), pl.ds(start_row(yy, zz, c), PIECE), :]

    def piece(xx, yy, zz):
        return pan.at[core, xx, pl.ds(start_row(yy, zz, core), PIECE), :]

    def unit_sem(yy, zz):
        return unit_recv.at[yy * NZ + zz]

    @pl.when(root)
    def _():
        def send_piece(i, carry):
            yy = lax.rem(i + 1, NY)
            k = i // NY
            zz = lax.rem(NZ + NZ // 2 + (1 - 2 * lax.rem(k, 2)) * ((k + 1) // 2), NZ)
            remote(
                a_ref.at[pl.ds(start_row(yy, zz, core), PIECE), :], piece(x, yy, zz),
                s1_send, s1_recv, device(x, yy, zz, core),
            ).start()
            return carry

        lax.fori_loop(0, NY * NZ - 1, send_piece, 0)
        mine = pltpu.make_async_copy(
            a_ref.at[pl.ds(start_row(0, 0, core), PIECE), :], piece(x, 0, 0), local_sem
        )
        mine.start()
        mine.wait()

    chunk = PW // CHUNKS
    base = row * PW
    other = wrap(xh + 1, 2)

    def far_rows(c, i):
        return own.at[pl.ds(pl.multiple_of((other * 2 + c) * PW + i * chunk, chunk), chunk), :]

    def send_far(i):
        remote(
            a_ref.at[pl.ds(pl.multiple_of(i * chunk, chunk), chunk), :],
            own.at[pl.ds(pl.multiple_of(base + i * chunk, chunk), chunk), :],
            e1_send, e1_recv.at[i], x_far,
        ).start()

    def pass_far(i):
        rows = far_rows(core, i)
        remote(rows, rows, e1_send, e1_recv.at[i], x_far).wait_recv()
        remote(rows, rows, e3_send, e3_recv.at[i], mate).start()

    def far_item(i):
        rows = far_rows(1 - core, i)
        remote(rows, rows, e3_send, e3_recv.at[i], mate).wait_recv()
        own_item(other, i)

    send_far(0)
    near = remote(a_ref, own.at[pl.ds(base, PW), :], e2_send, e2_recv, mate)
    near.start()
    keep = pltpu.make_async_copy(a_ref, own.at[pl.ds(base, PW), :], keep_sem)
    keep.start()
    for load in loads:
        load.wait()
    for i in range(4):
        high_parts[i], low_parts[i] = split(inverses[i // 2, i % 2])
    keep.wait()
    near.wait()

    def near_item(i, carry):
        own_item(xh, i)
        return carry

    lax.fori_loop(0, CHUNKS, near_item, 0)

    @pl.when(jnp.logical_not(root))
    def _():
        remote(piece(x, y, z), piece(x, y, z), s1_send, s1_recv, mate).wait_recv()

    for d in (1, 3, 2):
        remote(
            piece(x, y, z), piece(x, y, z), sx_send, sx_recv.at[d - 1],
            device(wrap(x + d, NX), y, z, core),
        ).start()
    send_far(1)
    pass_far(0)
    for d in (1, 3, 2):
        got = piece(wrap(x - d, NX), y, z)
        remote(got, got, sx_send, sx_recv.at[d - 1], mate).wait_recv()

    def send_z(yy, zz, d, c):
        ref = unit(yy, zz, c)
        remote(ref, ref, sz_send, unit_sem(yy, zz), device(x, y, wrap(z + d, NZ), c)).start()

    def send_y(ref, yy, zz, d, c):
        remote(ref, ref, sy_send, unit_sem(yy, zz), device(x, wrap(y + d, NY), z, c)).start()

    def send_mate(yy, zz, j, c):
        ref = unit(yy, zz, c)
        remote(ref, ref, swap_send, swap_recv.at[j], mate).start()

    def arrived(yy, zz, c):
        ref = unit(yy, zz, c)
        remote(ref, ref, sz_send, unit_sem(yy, zz), mate).wait_recv()

    def both_ways(zz, j):
        send_y(unit(y, zz, 0), y, zz, 1, 0)
        send_y(unit(y, zz, 0), y, zz, -1, 0)
        send_mate(y, zz, j, 0)

    order = [(0, y)] + [(k + 1, wrap(y + d, NY)) for k, d in enumerate((1, 3, 2))]

    @pl.when(core == 0)
    def _():
        send_z(y, z, 1, 0)
        send_z(y, z, -1, 0)
        both_ways(z, 0)

    @pl.when(core == 1)
    def _():
        send_z(y, z, 1, 1)
        send_z(y, z, -1, 1)
        for d in (1, 3, 2):
            send_y(unit(y, z, 1), y, z, d, 1)
        send_mate(y, z, 0, 1)
        for k, yy in order[1:]:
            arrived(yy, z, 1)
            send_z(yy, z, 1, 1)
            send_z(yy, z, -1, 1)
            send_mate(yy, z, 0, 1)

    def slot_core_0(t):
        @pl.when(t <= 7)
        def _():
            zz = nth(t)
            arrived(y, zz, 0)

            @pl.when((lax.rem(t, 2) == 1) & (t < 7))
            def _():
                send_z(y, zz, 1, 0)

            @pl.when((lax.rem(t, 2) == 0) & (t < 6))
            def _():
                send_z(y, zz, -1, 0)

            both_ways(zz, t)

        @pl.when((t >= LAG_1) & (t <= 7 + LAG_1))
        def _():
            zz = nth(t - LAG_1)
            yy = wrap(y - 1, NY)
            arrived(yy, zz, 0)
            send_y(half_unit(yy, zz, 0, 0), yy, zz, 1, 0)
            send_mate(yy, zz, t - LAG_1, 0)
            yy = wrap(y + 1, NY)
            arrived(yy, zz, 0)
            send_y(half_unit(yy, zz, 1, 0), yy, zz, -1, 0)
            send_mate(yy, zz, t - LAG_1, 0)

        @pl.when(t >= LAG)
        def _():
            zz = nth(t - LAG)
            yy = wrap(y + 2, NY)
            arrived(yy, zz, 0)
            send_mate(yy, zz, t - LAG, 0)

    def slot_core_1(t):
        zz = nth(t)
        up = lax.rem(t, 2) == 1
        for k, yy in order:
            arrived(yy, zz, 1)
            send_mate(yy, zz, t, 1)

            @pl.when(up & ((t < 5) | ((t == 5) & (k < 2))))
            def _():
                send_z(yy, zz, 1, 1)

            @pl.when(jnp.logical_not(up) & ((t < 6) | ((t == 6) & (k >= 2))))
            def _():
                send_z(yy, zz, -1, 1)

    def slot(t, carry):
        @pl.when(core == 0)
        def _():
            slot_core_0(t)

        @pl.when((core == 1) & (t <= 2))
        def _():
            slot_core_1(t)

        @pl.when((core == 1) & ((t == 5) | (t == 7)))
        def _():
            slot_core_1(t - 2)
            slot_core_1(t - 1)

        @pl.when((core == 1) & (t == 10))
        def _():
            slot_core_1(7)

        @pl.when((t == 2) | (t == 4))
        def _():
            send_far(t // 2 + 1)

        @pl.when((t == 5) | (t == 7) | (t == 9))
        def _():
            pass_far((t - 3) // 2)

        @pl.when(t >= LAG)
        def _():
            j = t - LAG
            ref = pan.at[1 - core, :, pl.ds(0, 64), :]
            remote(ref, ref, swap_send, swap_recv.at[j], mate).wait_recv()
            for b in (0, 1):
                panel_item(nth(j), b)

        @pl.when((t == 3) | (t == 6) | (t == 8) | (t == 10))
        def _():
            far_item((t - 1) // 2 - 1)

        @pl.when(t == 10)
        def _():
            solve_top()

        return carry

    lax.fori_loop(1, 8 + LAG, slot, 0)

    put((row == 1) & (col == 0), acc[PANEL_0_1])
    put((row > 1) & (col == 0), acc[PANEL_0_R])
    middle = acc[OWN_1] - dot3(split(acc[PANEL_0_1]), top())
    put((row == 1) & (col == 1), middle)
    middle = dot3_lower(lower1(), split(middle))
    put((row == 1) & (col > 1), middle)
    lower_cols = split(acc[PANEL_0_R])
    rest = acc[OWN_R] - dot3(lower_cols, top())
    panel_top = dot3_lower(lower0(), split(acc[PANEL_1_0]))
    lower_cols = acc[PANEL_1_R] - dot3(lower_cols, split(panel_top))
    lower_cols = dot3_upper(split(lower_cols), upper1())
    put((row > 1) & (col == 1), lower_cols)
    put((row > 1) & (col > 1), rest - dot3(split(lower_cols), split(middle)))

    def sent(sem, ref):
        remote(ref, ref, sem, s1_recv, mate).wait_send()

    block = own.at[pl.ds(0, PW), :]
    sent(sx_send, pan.at[0, pl.ds(0, 3), pl.ds(0, PIECE), :])
    sent(swap_send, pan.at[0])
    sent(e1_send, block)
    sent(e3_send, block)

    @pl.when(core == 0)
    def _():
        sent(sz_send, pan.at[0, :, pl.ds(0, PIECE * 7), :])
        sent(sy_send, pan.at[0, :, pl.ds(0, PIECE * 24), :])

    @pl.when(core == 1)
    def _():
        sent(sz_send, pan.at[1, :, pl.ds(0, PIECE * 28), :])
        sent(sy_send, pan.at[1, :, pl.ds(0, PIECE * 3), :])

    @pl.when(root)
    def _():
        sent(s1_send, pan.at[0, 0, pl.ds(0, PIECE * (NY * NZ - 1)), :])


def local(matrix, lower_inverses, upper_inverses, pivots):
    vmem = pl.BlockSpec(memory_space=pltpu.VMEM)
    dma = pltpu.SemaphoreType.DMA
    anywhere = pl.BlockSpec(memory_space=pl.ANY)
    return pl.pallas_call(
        kernel,
        out_shape=pltpu.VMEM((PW, PW), F32),
        in_specs=[anywhere, anywhere, anywhere, vmem],
        out_specs=vmem,
        scratch_shapes=[
            pltpu.VMEM((2, NX, PW, PW), F32),
            pltpu.VMEM((4 * PW, PW), F32),
            pltpu.VMEM((7, PW, PW), F32),
            pltpu.VMEM((2, 2, PW, PW), F32),
            pltpu.VMEM((5, PW, PW), BF16),
            pltpu.VMEM((5, PW, PW), BF16),
            pltpu.VMEM((3, PW, LANES), F32),
            dma, dma, dma, dma((3,)), dma, dma, dma((NY * NZ,)), dma, dma((NZ,)),
            dma, dma((CHUNKS,)), dma, dma, dma, dma((CHUNKS,)), dma, dma, dma((2,)),
        ],
        compiler_params=pltpu.CompilerParams(
            collective_id=0, has_side_effects=True, vmem_limit_bytes=56 * 2**20
        ),
        name="panels",
    )(matrix, lower_inverses, upper_inverses, pivots)


def solution(mesh):
    return jax.shard_map(
        local,
        mesh=mesh,
        in_specs=(P("row", "col"), P(), P(), P()),
        out_specs=P("row", "col"),
        check_vma=False,
    )
```

```python
import functools

import jax
import jax.numpy as jnp
from jax import lax
from jax.experimental import pallas as pl
from jax.experimental.pallas import tpu as pltpu
from jax.sharding import PartitionSpec as P

MESH = pl.DeviceIdType.MESH
PW = 512
NX, NY, NZ = 4, 4, 8
PIECE = 16
CHUNKS = 4
LANES = 128
LAG_1, LAG = 2, 4
OWN_0, OWN_1, OWN_R, PANEL_0_1, PANEL_0_R, PANEL_1_0, PANEL_1_R = range(7)
F32 = jnp.float32
BF16 = jnp.bfloat16


def split(value):
    high = value.astype(BF16)
    return high, (value - high.astype(F32)).astype(BF16)


def dot(a, b):
    return jnp.dot(a, b, preferred_element_type=F32)


def dot3(a, b):
    return dot(jnp.concatenate([a[0], a[0], a[1]], axis=1), jnp.concatenate([b[0], b[1], b[0]], axis=0))


def dot3_upper(a, b):
    h = PW // 2
    left = dot3([part[:, :h] for part in a], [part[:h, :h] for part in b])
    right = dot3(a, [part[:, h:] for part in b])
    return jnp.concatenate([left, right], axis=1)


def dot3_lower(a, b):
    h = PW // 2
    above = dot3([part[:h, :h] for part in a], [part[:h, :] for part in b])
    below = dot3([part[h:, :] for part in a], b)
    return jnp.concatenate([above, below], axis=0)


def device(x, y, z, core):
    return ((y * NZ + z) * 2 + lax.rem(x, 2), (x // 2) * 2 + core)


def wrap(value, size):
    return lax.rem(value + size, size)


def remote(src, dst, send, recv, target):
    return pltpu.make_async_remote_copy(
        src_ref=src, dst_ref=dst, send_sem=send, recv_sem=recv, device_id=target, device_id_type=MESH
    )


def column(row):
    shape = (PW, PW)
    eye = lax.broadcasted_iota(jnp.int32, shape, 0) == lax.broadcasted_iota(jnp.int32, shape, 1)
    return jnp.sum(jnp.where(eye, row, 0.0), axis=1, keepdims=True)


def swapped(rows, pivot_row, offset):
    lane = lax.broadcasted_iota(jnp.int32, (PW, PW), 1).astype(F32) + offset
    return rows + jnp.sum(jnp.where(pivot_row == rows, lane - rows, 0.0), axis=1, keepdims=True)


def kernel(
    a_ref, lower_ref, upper_ref, pivots_ref, o_ref,
    pan, own, acc, inverses, high_parts, low_parts, src,
    s1_send, s1_recv, sx_send, sx_recv, sz_send, sy_send, unit_recv, swap_send, swap_recv,
    e1_send, e1_recv, e2_send, e2_recv, e3_send, e3_recv, local_sem, keep_sem, inverse_sem,
):
    col = lax.axis_index("col")
    row = lax.axis_index("row")
    core = lax.rem(row, 2)
    xh = row // 2
    x = xh * 2 + lax.rem(col, 2)
    y = col // (2 * NZ)
    z = lax.rem(col // 2, NZ)
    root = (y == 0) & (z == 0)
    mate = device(x, y, z, 1 - core)
    x_far = device(wrap(x + 2, NX), y, z, core)

    partners = [mate]
    partners += [device(wrap(x + d, NX), y, z, core) for d in (1, 2, 3)]
    partners += [device(x, wrap(y + d, NY), z, core) for d in (1, 2, 3)]
    partners += [device(x, y, wrap(z + d, NZ), core) for d in (1, -1)]
    barrier = pltpu.get_barrier_semaphore()
    for partner in partners:
        pl.semaphore_signal(barrier, inc=1, device_id=partner, device_id_type=MESH)

    @pl.when(jnp.logical_not(root))
    def _():
        pl.semaphore_signal(barrier, inc=1, device_id=device(x, 0, 0, core), device_id_type=MESH)

    loads = [
        pltpu.make_async_copy(lower_ref, inverses.at[0], inverse_sem.at[0]),
        pltpu.make_async_copy(upper_ref, inverses.at[1], inverse_sem.at[1]),
    ]
    for load in loads:
        load.start()

    @pl.when(jnp.logical_not(root))
    def _():
        pl.semaphore_wait(barrier, len(partners))

    @pl.when(root)
    def _():
        pl.semaphore_wait(barrier, len(partners) + NY * NZ - 1)

    def inverse(i):
        return high_parts[i], low_parts[i]

    lower0, lower1, upper0, upper1, top = [functools.partial(inverse, i) for i in range(5)]

    def put(condition, value):
        @pl.when(condition)
        def _():
            o_ref[...] = value

    def solve_top():
        value = dot3_lower(lower0(), split(acc[OWN_0]))
        put((row == 0) & (col == 0), acc[OWN_0])
        put((row == 0) & (col > 0), value)
        high_parts[4], low_parts[4] = split(value)

    lane = lax.broadcasted_iota(jnp.int32, (1, LANES), 1)

    def take(values, ids, targets):
        high, low = split(values)
        for which, dst in targets:
            pick = jnp.concatenate(
                [jnp.where(src[which] == part.astype(F32), 1.0, 0.0).astype(BF16) for part in ids], axis=1
            )
            acc[dst] += dot(jnp.concatenate([pick, pick], axis=1), jnp.concatenate([high, low], axis=0))

    def own_item(half, i):
        start = half * 2 * PW + i * LANES
        starts = [pl.multiple_of(start + j * PW, LANES) for j in (0, 1)]
        values = jnp.concatenate([own[pl.ds(at, LANES), :] for at in starts], axis=0)
        take(values, [lane + at for at in starts], [(0, OWN_0), (1, OWN_1), (2, OWN_R)])

    def panel_item(zz, b):
        rows = [pl.multiple_of(yy * LANES + zz * PIECE, PIECE) for yy in range(NY)]
        parts = [pan[0, 2 * q + b, pl.ds(at, PIECE), :] for q in (0, 1) for at in rows]
        at = pl.multiple_of(zz * 64, 64)
        parts += [pan[1, 2 * q + b, pl.ds(at, 64), :] for q in (0, 1)]
        within = lax.rem(lane, 64)
        high = (lane // 64) * (2 * PW)
        ids = [
            high + (within // PIECE) * LANES + lax.rem(within, PIECE) + zz * PIECE,
            high + PW + within + zz * 64,
        ]
        targets = [(2, PANEL_0_R), (1, PANEL_0_1)] if b == 0 else [(2, PANEL_1_R), (0, PANEL_1_0)]
        values = jnp.concatenate(parts, axis=0)
        if b == 0:
            values = dot3_upper(split(values), upper0())
        take(values, ids, targets)

    def nth(j):
        return wrap(z + (1 - 2 * lax.rem(j, 2)) * ((j + 1) // 2), NZ)

    def start_row(yy, zz, c):
        return pl.multiple_of(PIECE * ((yy * NZ + zz) * (1 - c) + (zz * NY + yy) * c), PIECE)

    def unit(yy, zz, c):
        return pan.at[c, :, pl.ds(start_row(yy, zz, c), PIECE), :]

    def half_unit(yy, zz, h, c):
        return pan.at[c, pl.ds(2 * h, 2), pl.ds(start_row(yy, zz, c), PIECE), :]

    def piece(xx, yy, zz):
        return pan.at[core, xx, pl.ds(start_row(yy, zz, core), PIECE), :]

    def unit_sem(yy, zz):
        return unit_recv.at[yy * NZ + zz]

    @pl.when(root)
    def _():
        def send_piece(i, carry):
            yy = lax.rem(i + 1, NY)
            k = i // NY
            zz = lax.rem(NZ + NZ // 2 + (1 - 2 * lax.rem(k, 2)) * ((k + 1) // 2), NZ)
            remote(
                a_ref.at[pl.ds(start_row(yy, zz, core), PIECE), :], piece(x, yy, zz),
                s1_send, s1_recv, device(x, yy, zz, core),
            ).start()
            return carry

        lax.fori_loop(0, NY * NZ - 1, send_piece, 0)
        mine = pltpu.make_async_copy(
            a_ref.at[pl.ds(start_row(0, 0, core), PIECE), :], piece(x, 0, 0), local_sem
        )
        mine.start()
        mine.wait()

    chunk = PW // CHUNKS
    base = row * PW
    other = wrap(xh + 1, 2)

    def far_rows(c, i):
        return own.at[pl.ds(pl.multiple_of((other * 2 + c) * PW + i * chunk, chunk), chunk), :]

    def send_far(i):
        remote(
            a_ref.at[pl.ds(pl.multiple_of(i * chunk, chunk), chunk), :],
            own.at[pl.ds(pl.multiple_of(base + i * chunk, chunk), chunk), :],
            e1_send, e1_recv.at[i], x_far,
        ).start()

    def pass_far(i):
        rows = far_rows(core, i)
        remote(rows, rows, e1_send, e1_recv.at[i], x_far).wait_recv()
        remote(rows, rows, e3_send, e3_recv.at[i], mate).start()

    def far_item(i):
        rows = far_rows(1 - core, i)
        remote(rows, rows, e3_send, e3_recv.at[i], mate).wait_recv()
        own_item(other, i)

    send_far(0)
    near = remote(a_ref, own.at[pl.ds(base, PW), :], e2_send, e2_recv, mate)
    near.start()
    keep = pltpu.make_async_copy(a_ref, own.at[pl.ds(base, PW), :], keep_sem)
    keep.start()
    first = pivots_ref[0:1, :].astype(F32)
    second = pivots_ref[1:2, :].astype(F32)
    place = (lax.broadcasted_iota(jnp.int32, (PW, 1), 0) + row * PW).astype(F32)
    src[0] = jnp.broadcast_to(column(first), (PW, LANES))
    src[1] = jnp.broadcast_to(swapped(column(second), first, 0.0), (PW, LANES))
    src[2] = jnp.broadcast_to(swapped(swapped(place, second, float(PW)), first, 0.0), (PW, LANES))
    acc[...] = jnp.zeros(acc.shape, F32)
    for load in loads:
        load.wait()
    for i in range(4):
        high_parts[i], low_parts[i] = split(inverses[i // 2, i % 2])
    keep.wait()
    near.wait()

    def near_item(i, carry):
        own_item(xh, i)
        return carry

    lax.fori_loop(0, CHUNKS, near_item, 0)

    @pl.when(jnp.logical_not(root))
    def _():
        remote(piece(x, y, z), piece(x, y, z), s1_send, s1_recv, mate).wait_recv()

    for d in (2, 1, 3):
        remote(
            piece(x, y, z), piece(x, y, z), sx_send, sx_recv.at[d - 1],
            device(wrap(x + d, NX), y, z, core),
        ).start()
    send_far(1)
    pass_far(0)
    for d in (1, 3, 2):
        got = piece(wrap(x - d, NX), y, z)
        remote(got, got, sx_send, sx_recv.at[d - 1], mate).wait_recv()

    def send_z(yy, zz, d, c):
        ref = unit(yy, zz, c)
        remote(ref, ref, sz_send, unit_sem(yy, zz), device(x, y, wrap(z + d, NZ), c)).start()

    def send_y(ref, yy, zz, d, c):
        remote(ref, ref, sy_send, unit_sem(yy, zz), device(x, wrap(y + d, NY), z, c)).start()

    def send_mate(yy, zz, j, c):
        ref = unit(yy, zz, c)
        remote(ref, ref, swap_send, swap_recv.at[j], mate).start()

    def arrived(yy, zz, c):
        ref = unit(yy, zz, c)
        remote(ref, ref, sz_send, unit_sem(yy, zz), mate).wait_recv()

    def both_ways(zz, j):
        send_y(unit(y, zz, 0), y, zz, 1, 0)
        send_y(unit(y, zz, 0), y, zz, -1, 0)
        send_mate(y, zz, j, 0)

    order = [(0, y)] + [(k + 1, wrap(y + d, NY)) for k, d in enumerate((1, 3, 2))]

    @pl.when(core == 0)
    def _():
        send_z(y, z, 1, 0)
        send_z(y, z, -1, 0)
        both_ways(z, 0)

    @pl.when(core == 1)
    def _():
        send_z(y, z, 1, 1)
        send_z(y, z, -1, 1)
        for d in (1, 3, 2):
            send_y(unit(y, z, 1), y, z, d, 1)
        send_mate(y, z, 0, 1)
        for k, yy in order[1:]:
            arrived(yy, z, 1)
            send_z(yy, z, 1, 1)
            send_z(yy, z, -1, 1)
            send_mate(yy, z, 0, 1)

    def slot_core_0(t):
        @pl.when(t <= 7)
        def _():
            zz = nth(t)
            arrived(y, zz, 0)

            @pl.when((lax.rem(t, 2) == 1) & (t < 7))
            def _():
                send_z(y, zz, 1, 0)

            @pl.when((lax.rem(t, 2) == 0) & (t < 6))
            def _():
                send_z(y, zz, -1, 0)

            both_ways(zz, t)

        @pl.when((t >= LAG_1) & (t <= 7 + LAG_1))
        def _():
            zz = nth(t - LAG_1)
            yy = wrap(y - 1, NY)
            arrived(yy, zz, 0)
            send_y(half_unit(yy, zz, 0, 0), yy, zz, 1, 0)
            send_mate(yy, zz, t - LAG_1, 0)
            yy = wrap(y + 1, NY)
            arrived(yy, zz, 0)
            send_y(half_unit(yy, zz, 1, 0), yy, zz, -1, 0)
            send_mate(yy, zz, t - LAG_1, 0)

        @pl.when(t >= LAG)
        def _():
            zz = nth(t - LAG)
            yy = wrap(y + 2, NY)
            arrived(yy, zz, 0)
            send_mate(yy, zz, t - LAG, 0)

    def slot_core_1(t):
        zz = nth(t)
        up = lax.rem(t, 2) == 1
        for k, yy in order:
            arrived(yy, zz, 1)
            send_mate(yy, zz, t, 1)

            @pl.when(up & ((t < 5) | ((t == 5) & (k < 2))))
            def _():
                send_z(yy, zz, 1, 1)

            @pl.when(jnp.logical_not(up) & ((t < 6) | ((t == 6) & (k >= 2))))
            def _():
                send_z(yy, zz, -1, 1)

    def slot(t, carry):
        @pl.when(core == 0)
        def _():
            slot_core_0(t)

        @pl.when((core == 1) & (t <= 2))
        def _():
            slot_core_1(t)

        @pl.when((core == 1) & ((t == 5) | (t == 7)))
        def _():
            slot_core_1(t - 2)
            slot_core_1(t - 1)

        @pl.when((core == 1) & (t == 9))
        def _():
            slot_core_1(7)

        @pl.when((t == 2) | (t == 4))
        def _():
            send_far(t // 2 + 1)

        @pl.when((t == 5) | (t == 7) | (t == 9))
        def _():
            pass_far((t - 3) // 2)

        @pl.when(t >= LAG)
        def _():
            j = t - LAG
            ref = pan.at[1 - core, :, pl.ds(0, 64), :]
            remote(ref, ref, swap_send, swap_recv.at[j], mate).wait_recv()
            for b in (0, 1):
                panel_item(nth(j), b)

        @pl.when((t == 3) | (t == 6) | (t == 8) | (t == 10))
        def _():
            far_item((t - 1) // 2 - 1)

        @pl.when(t == 10)
        def _():
            solve_top()

        return carry

    lax.fori_loop(1, 8 + LAG, slot, 0)

    put((row == 1) & (col == 0), acc[PANEL_0_1])
    put((row > 1) & (col == 0), acc[PANEL_0_R])
    middle = acc[OWN_1] - dot3(split(acc[PANEL_0_1]), top())
    put((row == 1) & (col == 1), middle)
    middle = dot3_lower(lower1(), split(middle))
    put((row == 1) & (col > 1), middle)
    lower_cols = split(acc[PANEL_0_R])
    rest = acc[OWN_R] - dot3(lower_cols, top())
    panel_top = dot3_lower(lower0(), split(acc[PANEL_1_0]))
    lower_cols = acc[PANEL_1_R] - dot3(lower_cols, split(panel_top))
    lower_cols = dot3_upper(split(lower_cols), upper1())
    put((row > 1) & (col == 1), lower_cols)
    put((row > 1) & (col > 1), rest - dot3(split(lower_cols), split(middle)))

    def sent(sem, ref):
        remote(ref, ref, sem, s1_recv, mate).wait_send()

    block = own.at[pl.ds(0, PW), :]
    sent(sx_send, pan.at[0, pl.ds(0, 3), pl.ds(0, PIECE), :])
    sent(swap_send, pan.at[0])
    sent(e1_send, block)
    sent(e3_send, block)

    @pl.when(core == 0)
    def _():
        sent(sz_send, pan.at[0, :, pl.ds(0, PIECE * 7), :])
        sent(sy_send, pan.at[0, :, pl.ds(0, PIECE * 24), :])

    @pl.when(core == 1)
    def _():
        sent(sz_send, pan.at[1, :, pl.ds(0, PIECE * 28), :])
        sent(sy_send, pan.at[1, :, pl.ds(0, PIECE * 3), :])

    @pl.when(root)
    def _():
        sent(s1_send, pan.at[0, 0, pl.ds(0, PIECE * (NY * NZ - 1)), :])


def local(matrix, lower_inverses, upper_inverses, pivots):
    vmem = pl.BlockSpec(memory_space=pltpu.VMEM)
    dma = pltpu.SemaphoreType.DMA
    anywhere = pl.BlockSpec(memory_space=pl.ANY)
    return pl.pallas_call(
        kernel,
        out_shape=pltpu.VMEM((PW, PW), F32),
        in_specs=[anywhere, anywhere, anywhere, vmem],
        out_specs=vmem,
        scratch_shapes=[
            pltpu.VMEM((2, NX, PW, PW), F32),
            pltpu.VMEM((4 * PW, PW), F32),
            pltpu.VMEM((7, PW, PW), F32),
            pltpu.VMEM((2, 2, PW, PW), F32),
            pltpu.VMEM((5, PW, PW), BF16),
            pltpu.VMEM((5, PW, PW), BF16),
            pltpu.VMEM((3, PW, LANES), F32),
            dma, dma, dma, dma((3,)), dma, dma, dma((NY * NZ,)), dma, dma((NZ,)),
            dma, dma((CHUNKS,)), dma, dma, dma, dma((CHUNKS,)), dma, dma, dma((2,)),
        ],
        compiler_params=pltpu.CompilerParams(
            collective_id=0, has_side_effects=True, vmem_limit_bytes=56 * 2**20
        ),
        name="panels",
    )(matrix, lower_inverses, upper_inverses, pivots)


def solution(mesh):
    return jax.shard_map(
        local,
        mesh=mesh,
        in_specs=(P("row", "col"), P(), P(), P()),
        out_specs=P("row", "col"),
        check_vma=False,
    )
```
